32 devices in a mesh: dp: 4 (over y, x), ctx: 4 (over z), tensor: 2 (over core).
Axes of the slice: x: 2, y: 2, z: 4, core: 2. Of those that a mesh axis runs over, the one named last changes fastest.
Arguments:
- activations: bfloat16 [2, 8, 1024, 896], P(None, 'dp', 'ctx'), may hold values from -6 to 6
- segments: int32 [2, 8, 1024], P(None, 'dp', 'ctx'), may hold values from 0 to 20, as said below
- cotangent: bfloat16 [2, 8, 1024, 896], P(None, 'dp', 'ctx'), may hold values from -6 to 6
- query_weight: bfloat16 [896, 896], P(('dp', 'ctx'), 'tensor'), may hold values from -0.1875 to 0.1875
- key_weight: bfloat16 [896, 128], P(('dp', 'ctx'), 'tensor'), may hold values from -0.1875 to 0.1875
- value_weight: bfloat16 [896, 128], P(('dp', 'ctx'), 'tensor'), may hold values from -0.1875 to 0.1875
- out_weight: bfloat16 [896, 896], P('tensor', ('dp', 'ctx')), may hold values from -0.75 to 0.75
- query_bias: float32 [896], P('tensor'), may hold values from -3 to 3
- key_bias_vector: float32 [128], P('tensor'), may hold values from -3 to 3
- value_bias: float32 [128], P('tensor'), may hold values from -3 to 3
- attention_gain: float32 [896], replicated, may hold values from 0.1 to 1.9
- gate_weight: bfloat16 [896, 4864], P(('dp', 'ctx'), 'tensor'), may hold values from -0.1875 to 0.1875
- up_weight: bfloat16 [896, 4864], P(('dp', 'ctx'), 'tensor'), may hold values from -0.1875 to 0.1875
- down_weight: bfloat16 [4864, 896], P('tensor', ('dp', 'ctx')), may hold values from -0.078125 to 0.078125
- mlp_gain: float32 [896], replicated, may hold values from 0.1 to 1.9
Outputs:
- output: bfloat16 [2, 8, 1024, 896], P(None, 'dp', 'ctx')
- input_grad: float32 [2, 8, 1024, 896], P(None, 'dp', 'ctx')
- grad_query_weight: float32 [896, 896], P(('dp', 'ctx'), 'tensor')
- grad_key_weight: float32 [896, 128], P(('dp', 'ctx'), 'tensor')
- grad_value_weight: float32 [896, 128], P(('dp', 'ctx'), 'tensor')
- grad_out_weight: float32 [896, 896], P('tensor', ('dp', 'ctx'))
- grad_query_bias: float32 [896], P('tensor')
- grad_key_bias: float32 [128], P('tensor')
- grad_value_bias: float32 [128], P('tensor')
- grad_attention_gain: float32 [896], replicated
- grad_gate_weight: float32 [896, 4864], P(('dp', 'ctx'), 'tensor')
- grad_up_weight: float32 [896, 4864], P(('dp', 'ctx'), 'tensor')
- grad_down_weight: float32 [4864, 896], P('tensor', ('dp', 'ctx'))
- grad_mlp_gain: float32 [896], replicated
The draws below stay inside these ranges and needn't reach their ends.
Inputs may be any that keep to these rules, and one draw needn't show every extreme that they name: `segments`: within each sequence the numbers start at 0 and never fall. Every document except a sequence's last has 51 to 512 tokens. In each micro-batch, among the sequences of each index of dp, one holds a single document.
All inputs are finite; a program needn't handle non-finite values.
Results may differ from the reference program's by a relative error of at most 0.038.
Values may be sent and summed in bfloat16 or wider, within the bound.
No kernel may reach another device: no remote copies, remote signals or barrier semaphores. Data moves between devices by JAX's collectives and lax.ppermute only.
A program may use at most 192 MiB of HBM per device.

```python
import jax
import jax.numpy as jnp
from jax import lax

D = 896
HEADS = 14
KV_HEADS = 2
HEAD = 64
FF = 4864
MICRO = 2
SEQ_DP = 2
LENGTH = 1024
SEQS = 8
QW = 896
KVW = 128
N_DP = 4


def draw_segments(key, part):
    key = jax.random.fold_in(key, 11)
    total = MICRO * SEQS
    shortest = max(LENGTH // 20, 2)
    longest = LENGTH // 2
    slots = LENGTH // shortest + 1
    groups = MICRO * N_DP
    chosen = jax.random.randint(jax.random.fold_in(key, 2), (groups,), 0, SEQ_DP)
    flat = jnp.arange(total, dtype=jnp.int32)
    sizes = jax.random.randint(jax.random.fold_in(key, 1), (total, slots), shortest, longest + 1)
    if SEQ_DP > 1:
        densest = flat == (chosen[0] + 1) % SEQ_DP
        sizes = jnp.where(densest[:, None], shortest, sizes)
    ends = jnp.cumsum(sizes, axis=1)
    index = jnp.arange(LENGTH, dtype=jnp.int32)
    numbers = jnp.sum((ends[:, None, :] <= index[None, :, None]).astype(jnp.int32), axis=2)
    inner = flat % SEQS
    group_of = flat // SEQS * N_DP + inner // SEQ_DP
    single = chosen[group_of] == inner % SEQ_DP
    numbers = jnp.where(single[:, None], 0, numbers)
    return numbers.reshape(MICRO, SEQS, LENGTH).astype(jnp.int32)


def steps_of(key, extent, shards, least, top_value):
    def one(dim, blocks):
        draws = jax.random.uniform(jax.random.fold_in(jax.random.fold_in(key, 6), dim), (blocks,), jnp.float32, least / len(shards), top_value / len(shards))
        return jnp.repeat(jnp.exp(draws), extent[dim] // blocks).reshape((-1,) + (1,) * (len(extent) - dim - 1))

    loudness = one(*shards[0])
    for cut in shards[1:]:
        loudness = loudness * one(*cut)
    return loudness


def normal_values(rng, shape, scale, limit, split=(), kind=jnp.bfloat16):
    factor_of = steps_of(rng, shape, split, -0.22, 0.18) if split else 1.0
    entries = jax.random.normal(rng, shape, jnp.float32) * scale * factor_of
    return jnp.minimum(jnp.maximum(entries, -limit), limit).astype(kind)


def setup_inputs(seed: int = 0) -> dict:
    keys = jax.random.split(jax.random.key(seed), 16)
    activations = normal_values(keys[0], (MICRO, SEQS, LENGTH, D), 1.0, 6.0, ((1, 4), (2, 4)))
    segments = draw_segments(jax.random.fold_in(keys[15], 71), 0)
    cotangent = normal_values(keys[2], (MICRO, SEQS, LENGTH, D), 1.0, 6.0, ((1, 4), (2, 4)))
    query_weight = normal_values(keys[3], (D, QW), D ** -0.5, 0.1875, ((0, 16), (1, 2)))
    key_weight = normal_values(keys[4], (D, KVW), D ** -0.5, 0.1875, ((0, 16), (1, 2)))
    value_weight = normal_values(keys[5], (D, KVW), D ** -0.5, 0.1875, ((0, 16), (1, 2)))
    out_weight = normal_values(keys[6], (QW, D), (QW // 16) ** -0.5, 0.75, ((0, 2), (1, 16)))
    query_bias = normal_values(keys[7], (QW,), 0.5, 3.0, ((0, 2),), jnp.float32)
    key_bias_vector = normal_values(keys[8], (KVW,), 0.5, 3.0, ((0, 2),), jnp.float32)
    value_bias = normal_values(keys[9], (KVW,), 0.5, 3.0, ((0, 2),), jnp.float32)
    attention_gain = jnp.clip(1.0 + 0.18 * jax.random.normal(keys[10], (D,), jnp.float32), 0.1, 1.9)
    gate_weight = normal_values(keys[11], (D, FF), D ** -0.5, 0.1875, ((0, 16), (1, 2)))
    up_weight = normal_values(keys[12], (D, FF), D ** -0.5, 0.1875, ((0, 16), (1, 2)))
    down_weight = normal_values(keys[13], (FF, D), FF ** -0.5, 0.078125, ((0, 2), (1, 16)))
    mlp_gain = jnp.clip(1.0 + 0.18 * jax.random.normal(keys[14], (D,), jnp.float32), 0.1, 1.9)
    return dict(activations=activations, segments=segments, cotangent=cotangent, query_weight=query_weight, key_weight=key_weight, value_weight=value_weight, out_weight=out_weight, query_bias=query_bias, key_bias_vector=key_bias_vector, value_bias=value_bias, attention_gain=attention_gain, gate_weight=gate_weight, up_weight=up_weight, down_weight=down_weight, mlp_gain=mlp_gain)


@jax.custom_vjp
def low(v):
    return lax.optimization_barrier(v.astype(jnp.bfloat16)).astype(jnp.float32)

@jax.custom_vjp
def low_back(v):
    return v

def low_keep(v):
    return (low(v), None)

def low_pass(kept, grad):
    return (grad,)

def back_keep(v):
    return (v, None)

def back_low(kept, grad):
    return (low(grad),)
low.defvjp(low_keep, low_pass)
low_back.defvjp(back_keep, back_low)
HIGH = lax.Precision.HIGHEST
eps = 1e-06
theta = 1000000.0
masked = -1e+30

def matmul(left, right):
    return jnp.dot(left, right, precision=HIGH, preferred_element_type=jnp.float32)

def rms_unit(values):
    factor = lax.rsqrt(lax.optimization_barrier(jnp.mean(values * values, axis=-1, keepdims=True)) + eps)
    return values * factor

def positions_of(segment):
    index = jnp.arange(segment.shape[-1], dtype=jnp.int32)
    change = jnp.concatenate([jnp.ones(segment.shape[:-1] + (1,), jnp.bool_), segment[..., 1:] != segment[..., :-1]], axis=-1)
    starts = lax.cummax(jnp.where(change, index, 0), axis=segment.ndim - 1)
    return index - starts

def rotary_tables(position):
    half = HEAD // 2
    freq = theta ** (-(2.0 / HEAD) * jnp.arange(half, dtype=jnp.float32))
    angle = position.astype(jnp.float32)[..., None] * freq
    return (jnp.cos(angle), jnp.sin(angle))

def rotate(values, cosine, sine):
    half = values.shape[-1] // 2
    lower_half = values[..., :half]
    upper_half = values[..., half:]
    return jnp.concatenate([lower_half * cosine - upper_half * sine, upper_half * cosine + lower_half * sine], axis=-1)

def attention(query, key, value, segment):
    length = query.shape[0]
    group = HEADS // KV_HEADS
    block = min(512, length)
    count = length // block
    grouped = query.reshape(count, block, KV_HEADS, group, HEAD)
    starts = jnp.arange(count, dtype=jnp.int32) * block
    key_rows = jnp.arange(length, dtype=jnp.int32)
    scale = HEAD ** (-0.5)

    def one_block(item):
        part, start = item
        rows_now = start + jnp.arange(block, dtype=jnp.int32)
        ids_now = lax.dynamic_slice_in_dim(segment, start, block, 0)
        scores = jnp.einsum('qhgd,khd->hgqk', part, key, precision=HIGH) * scale
        scores = low_back(scores)
        allowed = (ids_now[:, None] == segment[None, :]) & (key_rows[None, :] <= rows_now[:, None])
        scores = jnp.where(allowed[None, None], scores, masked)
        weights = low(jax.nn.softmax(scores, axis=-1))
        return jnp.einsum('hgqk,khd->qhgd', weights, value, precision=HIGH)
    result = lax.map(jax.checkpoint(one_block), (grouped, starts))
    return result.reshape(length, HEADS * HEAD)

def layer(source, params, segment):
    query_weight, key_weight, value_weight, out_weight, query_bias, key_bias_vector, value_bias, attention_gain, gate_weight, up_weight, down_weight, mlp_gain = params
    length = source.shape[0]
    cosine, sine = rotary_tables(positions_of(segment))
    cosine = cosine[:, None, :]
    sine = sine[:, None, :]
    normed1 = low(rms_unit(source) * attention_gain)
    query = low_back(matmul(normed1, query_weight) + query_bias)
    key = low_back(matmul(normed1, key_weight) + key_bias_vector)
    value = low(low_back(matmul(normed1, value_weight) + value_bias))
    query = low(rotate(query.reshape(length, HEADS, HEAD), cosine, sine))
    key = low(rotate(key.reshape(length, KV_HEADS, HEAD), cosine, sine))
    value = value.reshape(length, KV_HEADS, HEAD)
    attended = low(low_back(attention(query, key, value, segment)))
    mixed = source + low_back(matmul(attended, out_weight))
    normed2 = low(rms_unit(mixed) * mlp_gain)
    gate = low_back(matmul(normed2, gate_weight))
    up_proj = low_back(matmul(normed2, up_weight))
    hidden = low(jax.nn.silu(gate) * up_proj)
    return mixed + low_back(matmul(hidden, down_weight))

def reference(activations, segments, cotangent, query_weight, key_weight, value_weight, out_weight, query_bias, key_bias_vector, value_bias, attention_gain, gate_weight, up_weight, down_weight, mlp_gain):
    params = tuple((w.astype(jnp.float32) for w in (query_weight, key_weight, value_weight, out_weight, query_bias, key_bias_vector, value_bias, attention_gain, gate_weight, up_weight, down_weight, mlp_gain)))
    inputs = activations.astype(jnp.float32).reshape(-1, LENGTH, D)
    id_rows = segments.reshape(-1, LENGTH)
    incoming_gradients = cotangent.astype(jnp.float32).reshape(-1, LENGTH, D)

    def visit(totals, item):
        source, segment, grad_out = item
        result, pull = jax.vjp(lambda values, weights: layer(values, weights, segment), source, params)
        grad_source, grad_params = pull(grad_out)
        totals = tuple((left + right for left, right in zip(totals, grad_params)))
        return (totals, (result.astype(jnp.bfloat16), grad_source))
    start = tuple((jnp.zeros_like(w) for w in params))
    totals, (results, grad_inputs) = lax.scan(visit, start, (inputs, id_rows, incoming_gradients))
    shape = activations.shape
    return (results.reshape(shape), grad_inputs.reshape(shape), totals[0], totals[1], totals[2], totals[3], totals[4], totals[5], totals[6], totals[7], totals[8], totals[9], totals[10], totals[11])
```

```python
import functools

import jax
import jax.numpy as jnp
from jax import lax
from jax.experimental import pallas as pl
from jax.experimental.pallas import tpu as pltpu
from jax.sharding import PartitionSpec as P

HEAD = 64

eps = 1e-06
theta = 1000000.0
masked = -1e30
f32 = jnp.float32
bf16 = jnp.bfloat16
VMEM_LIMIT = 56 * 1024 * 1024


def contract(left, right, dims):
    return lax.dot_general(left, right, ((dims[:1], dims[1:]), ((), ())), preferred_element_type=f32)


def swap(value, axis, size, bit):
    return lax.ppermute(value, axis, [(i, i ^ bit) for i in range(size)])


def tensor_sum(partial, size):
    sent = partial.astype(bf16)
    if size == 2:
        return sent.astype(f32) + swap(sent, "tensor", 2, 1).astype(f32)
    return lax.psum(sent, "tensor").astype(f32)


def place_kernel(where_ref, *refs):
    count = len(refs) - 2
    pieces, out_ref, sems = refs[:count], refs[count], refs[count + 1]
    copies = []
    for i in range(count):
        copies.append(pltpu.make_async_copy(pieces[i], out_ref.at[where_ref[i]], sems.at[i]))
    for copy in copies:
        copy.start()
    for copy in copies:
        copy.wait()


def place(pieces, where):
    count = len(pieces)
    return pl.pallas_call(
        place_kernel,
        out_shape=jax.ShapeDtypeStruct((count,) + pieces[0].shape, pieces[0].dtype),
        in_specs=[pl.BlockSpec(memory_space=pltpu.SMEM)] + [pl.BlockSpec(memory_space=pl.ANY)] * count,
        out_specs=pl.BlockSpec(memory_space=pltpu.VMEM),
        scratch_shapes=[pltpu.SemaphoreType.DMA((count,))],
        compiler_params=pltpu.CompilerParams(vmem_limit_bytes=VMEM_LIMIT),
    )(where, *pieces)


def gather_rows(shard, fast):
    if not fast:
        return lax.all_gather(shard, ("dp", "ctx"), axis=0, tiled=True)
    rows, width = shard.shape
    dp, ctx = lax.axis_index("dp"), lax.axis_index("ctx")
    other = swap(shard, "ctx", 4, 1)
    even = ctx % 2 == 0
    near = jnp.concatenate([jnp.where(even, shard, other), jnp.where(even, other, shard)], axis=0)
    far = swap(near, "ctx", 4, 2)
    near_1 = swap(near, "dp", 4, 1)
    near_2 = swap(near, "dp", 4, 2)
    near_3 = swap(near_1, "dp", 4, 2)
    far_2 = swap(far, "dp", 4, 2)
    far_1 = swap(far, "dp", 4, 1)
    far_3 = swap(far_2, "dp", 4, 1)
    half = ctx // 2
    spots = [(dp ^ k) * 2 + (half ^ h) for h in (0, 1) for k in (0, 1, 2, 3)]
    whole = place(
        [near, near_1, near_2, near_3, far, far_1, far_2, far_3], jnp.stack(spots).astype(jnp.int32)
    )
    return whole.reshape(16 * rows, width)


def pick(value, index, axis):
    return lax.dynamic_index_in_dim(value, index, axis, keepdims=False)


def add16(left, right):
    return (left.astype(f32) + right.astype(f32)).astype(bf16)


def scatter_rows(total, fast):
    total = total.astype(bf16)
    if not fast:
        return lax.psum_scatter(total, ("dp", "ctx"), scatter_dimension=0, tiled=True).astype(f32)
    rows, width = total.shape[0] // 16, total.shape[1]
    dp, ctx = lax.axis_index("dp"), lax.axis_index("ctx")
    y, x, half, odd = dp // 2, dp % 2, ctx // 2, ctx % 2
    cut = total.reshape(2, 2, 2, 2 * rows, width)
    first, second = cut[:, :, 0], cut[:, :, 1]
    first = add16(pick(first, y, 0), swap(pick(first, 1 - y, 0), "dp", 4, 2))
    second = add16(pick(second, x, 1), swap(pick(second, 1 - x, 1), "dp", 4, 1))
    first = add16(pick(first, x, 0), swap(pick(first, 1 - x, 0), "dp", 4, 1))
    second = add16(pick(second, y, 0), swap(pick(second, 1 - y, 0), "dp", 4, 2))
    low = half == 0
    both = add16(
        jnp.where(low, first, second), swap(jnp.where(low, second, first), "ctx", 4, 2)
    ).reshape(2, rows, width)
    return pick(both, odd, 0).astype(f32) + swap(pick(both, 1 - odd, 0), "ctx", 4, 1).astype(f32)


def sum_small(value, fast):
    if not fast:
        return lax.psum(value, ("dp", "ctx"))
    for axis, bit in (("ctx", 1), ("ctx", 2), ("dp", 1), ("dp", 2)):
        value = value + swap(value, axis, 4, bit)
    return value


def earlier(value, ctx_size):
    blocks = [value]
    for back in range(1, ctx_size):
        blocks.append(lax.ppermute(value, "ctx", [(i, i + back) for i in range(ctx_size - back)]))
    return jnp.concatenate(blocks, axis=-1)


def give_back(value, ctx_size):
    stretch = value.shape[-1] // ctx_size
    total = value[..., :stretch].astype(f32)
    for back in range(1, ctx_size):
        block = value[..., back * stretch : (back + 1) * stretch]
        total = total + lax.ppermute(
            block, "ctx", [(i + back, i) for i in range(ctx_size - back)]
        ).astype(f32)
    return total


def set_up(keys, queries, bias):
    info = keys[0].T
    allowed = (info[:, 0:1] == queries[0, 0:1]) & (info[:, 1:2] <= queries[0, 1:2])
    bias[...] = jnp.where(allowed, 0.0, masked)


def turned(value):
    return value.astype(f32).T.astype(bf16)


def forward_kernel(q_ref, kv_ref, keys, queries, out_ref, log_ref, bias, key):
    @pl.when(pl.program_id(1) == 0)
    def _():
        set_up(keys, queries, bias)
        key[...] = turned(kv_ref[:HEAD, :])

    scores = jnp.dot(key[...], q_ref[...], preferred_element_type=f32) + bias[...]
    top = jnp.max(scores, axis=0, keepdims=True)
    weights = jnp.exp(scores - top)
    total = jnp.sum(weights, axis=0, keepdims=True)
    summed = jnp.dot(kv_ref[HEAD:, :], weights.astype(bf16), preferred_element_type=f32)
    out_ref[...] = (summed / total).astype(bf16)
    log_ref[0, 0] = top + jnp.log(total)


def backward_kernel(
    q_ref, do_ref, out_ref, log_ref, kv_ref, keys, queries, dq_ref, dkv_ref, bias, key, val, acc
):
    head = pl.program_id(1)

    @pl.when(head == 0)
    def _():
        set_up(keys, queries, bias)
        key[...] = turned(kv_ref[:HEAD, :])
        val[...] = turned(kv_ref[HEAD:, :])
        acc[...] = jnp.zeros_like(acc)

    query, grad = q_ref[...], do_ref[...]
    scores = jnp.dot(key[...], query, preferred_element_type=f32) + bias[...]
    prob = jnp.exp(scores - log_ref[0, 0])
    delta = jnp.sum(grad.astype(f32) * out_ref[...].astype(f32), axis=0, keepdims=True)
    grad_prob = jnp.dot(val[...], grad, preferred_element_type=f32)
    grad_score = (prob * (grad_prob - delta)).astype(bf16)
    dq_ref[...] = jnp.dot(kv_ref[:HEAD, :], grad_score, preferred_element_type=f32)
    acc[:HEAD, :] += contract(query, grad_score, (1, 1))
    acc[HEAD:, :] += contract(grad, prob.astype(bf16), (1, 1))

    @pl.when(head == pl.num_programs(1) - 1)
    def _():
        dkv_ref[...] = acc[...].astype(bf16)


def attention_specs(stretch, length):
    head_block = pl.BlockSpec((HEAD, stretch), lambda s, h: (h, s))
    log_block = pl.BlockSpec((1, 1, 1, stretch), lambda s, h: (s, h, 0, 0))
    kv_block = pl.BlockSpec((2 * HEAD, length), lambda s, h: (0, s))
    key_block = pl.BlockSpec((1, 8, length), lambda s, h: (s, 0, 0))
    query_block = pl.BlockSpec((1, 8, stretch), lambda s, h: (s, 0, 0))
    return head_block, log_block, kv_block, [key_block, query_block]


def attention_forward(query, pair, ids, stretch, length):
    seqs, group = query.shape[1] // stretch, query.shape[0] // HEAD
    head_block, log_block, kv_block, id_blocks = attention_specs(stretch, length)
    return pl.pallas_call(
        forward_kernel,
        grid=(seqs, group),
        in_specs=[head_block, kv_block] + id_blocks,
        out_specs=[head_block, log_block],
        out_shape=[
            jax.ShapeDtypeStruct(query.shape, bf16),
            jax.ShapeDtypeStruct((seqs, group, 1, stretch), f32),
        ],
        scratch_shapes=[pltpu.VMEM((length, stretch), f32), pltpu.VMEM((length, HEAD), bf16)],
        compiler_params=pltpu.CompilerParams(vmem_limit_bytes=VMEM_LIMIT),
    )(query, pair, *ids)


def attention_backward(query, grad, attended, logsum, pair, ids, stretch, length):
    seqs, group = query.shape[1] // stretch, query.shape[0] // HEAD
    head_block, log_block, kv_block, id_blocks = attention_specs(stretch, length)
    return pl.pallas_call(
        backward_kernel,
        grid=(seqs, group),
        in_specs=[head_block, head_block, head_block, log_block, kv_block] + id_blocks,
        out_specs=[head_block, kv_block],
        out_shape=[
            jax.ShapeDtypeStruct(query.shape, f32),
            jax.ShapeDtypeStruct(pair.shape, bf16),
        ],
        scratch_shapes=[
            pltpu.VMEM((length, stretch), f32),
            pltpu.VMEM((length, HEAD), bf16),
            pltpu.VMEM((length, HEAD), bf16),
            pltpu.VMEM((2 * HEAD, length), f32),
        ],
        compiler_params=pltpu.CompilerParams(vmem_limit_bytes=VMEM_LIMIT),
    )(query, grad, attended, logsum, pair, *ids)


def turn(values, cosine, sine, sign):
    feats, tokens = values.shape
    parts = values.reshape(feats // HEAD, 2, HEAD // 2, tokens)
    a, b = parts[:, 0], parts[:, 1]
    s = sine * sign
    return jnp.stack([a * cosine - b * s, b * cosine + a * s], axis=1).reshape(feats, tokens)


def norm_grad(grad, gain, unit, inverse):
    scaled = grad * gain
    return inverse * (scaled - unit * jnp.mean(scaled * unit, axis=-1, keepdims=True))


def local(
    sizes,
    activations,
    segments,
    cotangent,
    query_weight,
    key_weight,
    value_weight,
    out_weight,
    query_bias,
    key_bias_vector,
    value_bias,
    attention_gain,
    gate_weight,
    up_weight,
    down_weight,
    mlp_gain,
):
    dp_size, ctx_size, tensor_size = sizes
    fast = dp_size == 4 and ctx_size == 4
    near_keys = ctx_size <= 4
    micros, per_micro, stretch, width = activations.shape
    seqs = micros * per_micro
    tokens = seqs * stretch
    length = ctx_size * stretch
    qw = query_weight.shape[1]
    units = gate_weight.shape[1]
    scale = HEAD ** (-0.5)
    ctx = lax.axis_index("ctx")

    qkv_shard = jnp.concatenate([query_weight, key_weight, value_weight], axis=1)
    w_qkv = gather_rows(qkv_shard, fast)
    w_out = gather_rows(out_weight.T, fast)
    w_gate = gather_rows(gate_weight, fast)
    w_up = gather_rows(up_weight, fast)
    w_down = gather_rows(down_weight.T, fast)

    own_ids = segments.reshape(seqs, stretch)
    steps = jnp.arange(stretch, dtype=jnp.int32)
    query_pos = ctx * stretch + steps
    if near_keys:
        key_pos = jnp.concatenate([(ctx - r) * stretch + steps for r in range(ctx_size)])
        key_ids = jnp.where(key_pos >= 0, earlier(own_ids, ctx_size), -1)
    else:
        key_pos = jnp.arange(length, dtype=jnp.int32)
        key_ids = lax.all_gather(own_ids, "ctx", axis=1, tiled=True)
    before = (key_ids[:, :, None] == own_ids[:, None, :]) & (
        key_pos[None, :, None] < query_pos[None, None, :]
    )
    position = jnp.sum(before.astype(f32), axis=1).reshape(1, tokens)
    freq = theta ** (-(2.0 / HEAD) * jnp.arange(HEAD // 2, dtype=f32))
    angle = freq[:, None] * position
    cosine, sine = jnp.cos(angle), jnp.sin(angle)
    ids = tuple(
        jnp.concatenate(
            [number[:, None], jnp.broadcast_to(place_of, number.shape)[:, None]] + [number[:, None]] * 6, axis=1
        ).astype(f32)
        for number, place_of in ((key_ids, key_pos), (own_ids, query_pos))
    )

    source = activations.reshape(tokens, width).astype(f32)
    inverse1 = lax.rsqrt(jnp.mean(source * source, axis=-1, keepdims=True) + eps)
    unit1 = source * inverse1
    normed1 = (unit1 * attention_gain).astype(bf16)
    bias = jnp.concatenate([query_bias, key_bias_vector, value_bias])
    qkv = contract(w_qkv, normed1, (0, 1)) + bias[:, None]
    query = (turn(qkv[:qw], cosine, sine, 1.0).astype(bf16) * scale).astype(bf16)
    key = turn(qkv[qw : qw + HEAD], cosine, sine, 1.0).astype(bf16)
    pair = jnp.concatenate([key, qkv[qw + HEAD :].astype(bf16)], axis=0)

    def group_of(value, m):
        wide = value.shape[1] // micros
        return value[:, m * wide : (m + 1) * wide]

    def ids_of(m):
        return tuple(v[m * per_micro : (m + 1) * per_micro] for v in ids)

    pairs, attended, logsums = [], [], []
    for m in range(micros):
        mine = group_of(pair, m).reshape(2 * HEAD, per_micro, stretch)
        if near_keys:
            wide = earlier(mine, ctx_size)
        else:
            wide = lax.all_gather(mine, "ctx", axis=2, tiled=True)
        pairs.append(wide.reshape(2 * HEAD, per_micro * length))
    for m in range(micros):
        out, logsum = attention_forward(group_of(query, m), pairs[m], ids_of(m), stretch, length)
        attended.append(out)
        logsums.append(logsum)
    partial = jnp.concatenate([contract(out, w_out, (0, 1)) for out in attended], axis=0)
    mixed = source + tensor_sum(partial, tensor_size)

    inverse2 = lax.rsqrt(jnp.mean(mixed * mixed, axis=-1, keepdims=True) + eps)
    unit2 = mixed * inverse2
    normed2 = (unit2 * mlp_gain).astype(bf16)
    gate = contract(normed2, w_gate, (1, 0))
    up_proj = contract(normed2, w_up, (1, 0))
    sigma = jax.nn.sigmoid(gate)
    silu = gate * sigma
    hidden = (silu * up_proj).astype(bf16)
    result = mixed + tensor_sum(contract(hidden, w_down, (1, 1)), tensor_size)
    output = result.astype(bf16).reshape(activations.shape)

    grad_branch = cotangent.reshape(tokens, width)
    grad_result = grad_branch.astype(f32)
    grad_down = scatter_rows(contract(grad_branch, hidden, (0, 0)), fast)
    grad_hidden = contract(grad_branch, w_down, (1, 0))
    grad_gate = (grad_hidden * up_proj * sigma * (1.0 + gate * (1.0 - sigma))).astype(bf16)
    grad_up = (grad_hidden * silu).astype(bf16)
    grad_gate_w = scatter_rows(contract(normed2, grad_gate, (0, 0)), fast)
    grad_up_w = scatter_rows(contract(normed2, grad_up, (0, 0)), fast)
    grad_normed2 = tensor_sum(
        contract(grad_gate, w_gate, (1, 1)) + contract(grad_up, w_up, (1, 1)), tensor_size
    )
    grad_gain2 = jnp.sum(grad_normed2 * unit2, axis=0)
    grad_mixed = grad_result + norm_grad(grad_normed2, mlp_gain, unit2, inverse2)

    grad_attn = grad_mixed.astype(bf16)
    grad_out_w = jnp.zeros((width, qw), f32)
    grad_queries, grad_pairs = [], []
    for m in range(micros):
        rows = tokens // micros
        grad_attn_now = grad_attn[m * rows : (m + 1) * rows]
        grad_out_w = grad_out_w + contract(grad_attn_now, attended[m], (0, 1))
        grad_attended = contract(w_out, grad_attn_now, (0, 1)).astype(bf16)
        grad_query, grad_wide = attention_backward(
            group_of(query, m), grad_attended, attended[m], logsums[m], pairs[m], ids_of(m), stretch, length
        )
        grad_wide = grad_wide.reshape(2 * HEAD, per_micro, length)
        if near_keys:
            own = give_back(grad_wide, ctx_size)
        else:
            own = lax.psum_scatter(grad_wide, "ctx", scatter_dimension=2, tiled=True).astype(f32)
        grad_queries.append(grad_query)
        grad_pairs.append(own.reshape(2 * HEAD, per_micro * stretch))
    grad_query = jnp.concatenate(grad_queries, axis=1) * scale
    grad_pair = jnp.concatenate(grad_pairs, axis=1)
    grad_qkv = jnp.concatenate(
        [
            turn(grad_query, cosine, sine, -1.0),
            turn(grad_pair[:HEAD], cosine, sine, -1.0),
            grad_pair[HEAD:],
        ],
        axis=0,
    ).astype(bf16)
    grad_bias = jnp.sum(grad_qkv.astype(f32), axis=1)
    grad_out_w = scatter_rows(grad_out_w, fast)
    grad_qkv_w = scatter_rows(contract(normed1, grad_qkv, (0, 1)), fast)
    grad_normed1 = tensor_sum(contract(grad_qkv, w_qkv, (0, 1)), tensor_size)
    grad_gain1 = jnp.sum(grad_normed1 * unit1, axis=0)
    grad_source = grad_mixed + norm_grad(grad_normed1, attention_gain, unit1, inverse1)

    smalls = sum_small(jnp.concatenate([grad_bias, grad_gain1, grad_gain2]), fast)
    ends = [qw, qw + HEAD, qw + 2 * HEAD, qw + 2 * HEAD + width]
    small = jnp.split(smalls, ends)
    return (
        output,
        grad_source.reshape(activations.shape),
        grad_qkv_w[:, :qw],
        grad_qkv_w[:, qw : qw + HEAD],
        grad_qkv_w[:, qw + HEAD :],
        grad_out_w.T,
        small[0],
        small[1],
        small[2],
        small[3],
        grad_gate_w,
        grad_up_w,
        grad_down.T,
        small[4],
    )


def solution(mesh):
    sizes = (mesh.shape["dp"], mesh.shape["ctx"], mesh.shape["tensor"])
    return jax.shard_map(
        functools.partial(local, sizes),
        mesh=mesh,
        in_specs=(
            P(None, "dp", "ctx", None),
            P(None, "dp", "ctx"),
            P(None, "dp", "ctx", None),
            P(("dp", "ctx"), "tensor"),
            P(("dp", "ctx"), "tensor"),
            P(("dp", "ctx"), "tensor"),
            P("tensor", ("dp", "ctx")),
            P("tensor"),
            P("tensor"),
            P("tensor"),
            P(),
            P(("dp", "ctx"), "tensor"),
            P(("dp", "ctx"), "tensor"),
            P("tensor", ("dp", "ctx")),
            P(),
        ),
        out_specs=(
            P(None, "dp", "ctx", None),
            P(None, "dp", "ctx", None),
            P(("dp", "ctx"), "tensor"),
            P(("dp", "ctx"), "tensor"),
            P(("dp", "ctx"), "tensor"),
            P("tensor", ("dp", "ctx")),
            P("tensor"),
            P("tensor"),
            P("tensor"),
            P(),
            P(("dp", "ctx"), "tensor"),
            P(("dp", "ctx"), "tensor"),
            P("tensor", ("dp", "ctx")),
            P(),
        ),
        check_vma=False,
    )
```

```python
import functools

import jax
import jax.numpy as jnp
from jax import lax
from jax.experimental import pallas as pl
from jax.experimental.pallas import tpu as pltpu
from jax.sharding import PartitionSpec as P

HEAD = 64

eps = 1e-06
theta = 1000000.0
masked = -1e30
f32 = jnp.float32
bf16 = jnp.bfloat16
VMEM_LIMIT = 56 * 1024 * 1024


def contract(left, right, dims):
    return lax.dot_general(left, right, ((dims[:1], dims[1:]), ((), ())), preferred_element_type=f32)


def swap(value, axis, size, bit):
    return lax.ppermute(value, axis, [(i, i ^ bit) for i in range(size)])


def tensor_sum(partial, size):
    sent = partial.astype(bf16)
    if size == 2:
        return sent.astype(f32) + swap(sent, "tensor", 2, 1).astype(f32)
    return lax.psum(sent, "tensor").astype(f32)


def pair_of(dp, ctx):
    return dp * 2 + ctx // 2


def hold(value, held, names):
    names = [name for name in names if name in held]
    value, *got = lax.optimization_barrier((value,) + tuple(held[name] for name in names))
    held.update(zip(names, got))
    return value


def gather_whole(shard):
    return lax.all_gather(shard, ("dp", "ctx"), axis=0, tiled=True)


def scatter_whole(total):
    return lax.psum_scatter(total, ("dp", "ctx"), scatter_dimension=0, tiled=True).astype(f32)


def gather_begin(shard):
    held = {"z%d" % k: swap(shard, "ctx", 4, k) for k in (1, 2, 3)}
    held["own"] = shard
    return held


BLOCKS = ("near", "near1", "near2", "near3", "far", "far1", "far2", "far3")


def gather_next(held, *names):
    def in_order(one, two):
        even = lax.axis_index("ctx") % 2 == 0
        return jnp.concatenate([jnp.where(even, one, two), jnp.where(even, two, one)], axis=0)

    for name in names:
        if name in held:
            continue
        if name == "near":
            held[name] = in_order(held["own"], held["z1"])
        elif name == "far":
            held[name] = in_order(held["z2"], held["z3"])
        else:
            source, bit = {
                "near1": ("near", 1),
                "near2": ("near", 2),
                "near3": ("near1", 2),
                "far1": ("far", 1),
                "far2": ("far", 2),
                "far3": ("far2", 1),
            }[name]
            held[name] = swap(held[source], "dp", 4, bit)


def gather_end(held):
    gather_next(held, *BLOCKS)
    return [held[name] for name in BLOCKS]


def gathered_spots():
    me = pair_of(lax.axis_index("dp"), lax.axis_index("ctx"))
    return jnp.stack([me ^ (k * 2 + h) for h in (0, 1) for k in (0, 1, 2, 3)]).astype(jnp.int32)


def kept_spots():
    me = pair_of(lax.axis_index("dp"), lax.axis_index("ctx"))
    order = (0, 2, 4, 6, 1, 5, 3, 7)
    return jnp.stack([me ^ r for r in order]).astype(jnp.int32)


def place_kernel(where_ref, *refs):
    count = len(refs) - 2
    pieces, out_ref, sems = refs[:count], refs[count], refs[count + 1]
    copies = [
        pltpu.make_async_copy(pieces[i], out_ref.at[where_ref[i]], sems.at[i]) for i in range(count)
    ]
    for copy in copies:
        copy.start()
    for copy in copies:
        copy.wait()


def place(pieces, where):
    count = len(pieces)
    whole = pl.pallas_call(
        place_kernel,
        out_shape=jax.ShapeDtypeStruct((count,) + pieces[0].shape, pieces[0].dtype),
        in_specs=[pl.BlockSpec(memory_space=pltpu.SMEM)] + [pl.BlockSpec(memory_space=pl.ANY)] * count,
        out_specs=pl.BlockSpec(memory_space=pltpu.VMEM),
        scratch_shapes=[pltpu.SemaphoreType.DMA((count,))],
        compiler_params=pltpu.CompilerParams(vmem_limit_bytes=VMEM_LIMIT),
    )(where, *pieces)
    return whole.reshape(count * pieces[0].shape[0], pieces[0].shape[1])


def add16(left, right):
    return (left.astype(f32) + right.astype(f32)).astype(bf16)


def scatter_begin(parts):
    keep_a, send_a, keep_b, send_b = parts
    return {"keep": (keep_a, keep_b), "a1": swap(send_a, "dp", 4, 2), "b1": swap(send_b, "dp", 4, 1)}


def scatter_second(held):
    keep_a, keep_b = held["keep"]
    a, b = held["a1"], held["b1"]
    held["a2"] = swap(add16(keep_a[1], a[1]), "dp", 4, 1)
    held["b2"] = swap(add16(keep_b[1], b[1]), "dp", 4, 2)
    held["left"] = add16(keep_a[0], a[0]), add16(keep_b[0], b[0])


def scatter_third(held):
    left_a, left_b = held["left"]
    near, far = add16(left_a, held["a2"]), add16(left_b, held["b2"])
    odd = lax.axis_index("ctx") % 2

    def half_of(value, at):
        rows = value.shape[0] // 2
        return lax.dynamic_slice_in_dim(value, at * rows, rows, 0)

    held["mine"] = half_of(near, odd)
    held["c1"] = swap(half_of(near, 1 - odd), "ctx", 4, 1)
    held["c2"] = swap(half_of(far, odd), "ctx", 4, 2)
    held["c3"] = swap(half_of(far, 1 - odd), "ctx", 4, 3)


def scatter_end(held):
    if "a2" not in held:
        scatter_second(held)
    if "c1" not in held:
        scatter_third(held)
    total = held["mine"].astype(f32)
    for name in ("c1", "c2", "c3"):
        total = total + held[name].astype(f32)
    return total


def in_parts(total):
    cut, spots = total.astype(bf16).reshape(8, -1, total.shape[1]), kept_spots()
    block = [lax.dynamic_index_in_dim(cut, spots[i], 0) for i in range(8)]
    return [jnp.concatenate(block[2 * i : 2 * i + 2]) for i in range(4)]


def sum_small(value, fast):
    if not fast:
        return lax.psum(value, ("dp", "ctx"))
    for axis, bit in (("ctx", 1), ("ctx", 2), ("dp", 1), ("dp", 2)):
        value = value + swap(value, axis, 4, bit)
    return value


def earlier(value, ctx_size):
    return [value] + [
        lax.ppermute(value, "ctx", [(i, i + back) for i in range(ctx_size - back)])
        for back in range(1, ctx_size)
    ]


def give_back(blocks, ctx_size):
    total = blocks[0].astype(f32)
    for back in range(1, ctx_size):
        total = total + lax.ppermute(
            blocks[back], "ctx", [(i + back, i) for i in range(ctx_size - back)]
        ).astype(f32)
    return total


def units_kernel(counts, parts, has_base, outs, where, spots, x_ref, dy_ref, xt_ref, dyt_ref, *refs):
    pieces, refs = refs[: sum(parts)], refs[sum(parts) :]
    if has_base:
        base, refs = refs[:2], refs[2:]
    out_ref, dn_ref, *refs = refs
    grads, refs = refs[:outs], refs[outs:]
    if has_base:
        (acc_out, acc_dn), refs = refs[:2], refs[2:]
    else:
        acc_out, acc_dn = out_ref, dn_ref
    weights, xt, dyt, sems = refs
    count = sum(counts)
    moves = []
    for i in range(8):
        moves.append((xt_ref.at[spots[i]], xt.at[i]))
        moves.append((dyt_ref.at[spots[i]], dyt.at[i]))
    taken, begin = 0, 0
    for part, units in zip(parts, counts):
        for m in range(3):
            there, here = pl.ds(m * units, units), pl.ds(m * count + begin, units)
            for i in range(part):
                if part == 1:
                    moves.append((pieces[taken].at[:, :, there], weights.at[:, :, here]))
                else:
                    moves.append((pieces[taken + i].at[:, there], weights.at[where[i], :, here]))
        taken, begin = taken + part, begin + units
    copies = [pltpu.make_async_copy(a, b, sems.at[i]) for i, (a, b) in enumerate(moves)]
    for copy in copies:
        copy.start()
    if has_base:
        acc_out[...] = base[0][...]
        acc_dn[...] = base[1][...]
    else:
        acc_out[...] = jnp.zeros_like(acc_out)
        acc_dn[...] = jnp.zeros_like(acc_dn)
    for copy in copies:
        copy.wait()
    depth = x_ref.shape[1]

    def weight(m, start, size):
        return weights[:, :, pl.ds(m * count + start, size)].reshape(depth, size)

    def some_units(start, size):
        w_gate, w_up, w_down = (weight(m, start, size) for m in range(3))
        gate = jnp.dot(x_ref[...], w_gate, preferred_element_type=f32)
        up = jnp.dot(x_ref[...], w_up, preferred_element_type=f32)
        d_hidden = jnp.dot(dy_ref[...], w_down, preferred_element_type=f32)
        sigma = jax.nn.sigmoid(gate)
        silu = gate * sigma
        hidden = (silu * up).astype(bf16)
        d_gate = (d_hidden * up * (sigma * (1.0 + gate * (1.0 - sigma)))).astype(bf16)
        d_up = (d_hidden * silu).astype(bf16)
        acc_out[...] += contract(hidden, w_down, (1, 1))
        acc_dn[...] += contract(d_gate, w_gate, (1, 1)) + contract(d_up, w_up, (1, 1))
        for m, (left, right) in enumerate(((xt, d_gate), (xt, d_up), (dyt, hidden))):
            grad = jnp.dot(
                left[...].reshape(depth, left.shape[2]), right, preferred_element_type=f32
            ).astype(bf16).reshape(8, depth // 8, size)
            for i, grad_ref in enumerate(grads):
                each = 8 // outs
                grad_ref[:, :, pl.ds(m * count + start, size)] = grad[each * i : each * i + each]

    wide = UNIT_TILE
    full = count // wide

    @pl.loop(0, full)
    def _(step):
        some_units(pl.multiple_of(step * wide, 128), wide)

    if count % wide:
        some_units(full * wide, count % wide)
    if has_base:
        out_ref[...] = acc_out[...].astype(out_ref.dtype)
        dn_ref[...] = acc_dn[...].astype(dn_ref.dtype)


UNIT_TILE = 256
SHARES = (8,)


def some_units(packs, where, spots, x, dy, xt, dyt, base, outs):
    tokens, depth = x.shape
    rows = depth // 8
    counts = [pack[0].shape[-1] // 3 for pack in packs]
    parts = [len(pack) for pack in packs]
    pieces = [piece for pack in packs for piece in pack]
    wide = 3 * sum(counts)
    whole = pl.BlockSpec(memory_space=pltpu.VMEM)
    smem = pl.BlockSpec(memory_space=pltpu.SMEM)
    anywhere = pl.BlockSpec(memory_space=pl.ANY)
    has_base = base is not None
    sums = jax.ShapeDtypeStruct((tokens, depth), bf16 if has_base else f32)
    grad = jax.ShapeDtypeStruct((8 // outs, rows, wide), bf16)
    scratch = [pltpu.VMEM((tokens, depth), f32)] * 2 if has_base else []
    return pl.pallas_call(
        functools.partial(units_kernel, counts, parts, has_base, outs),
        out_shape=[sums, sums] + [grad] * outs,
        in_specs=[smem, smem, whole, whole] + [anywhere] * (2 + len(pieces)) + ([whole] * 2 if has_base else []),
        out_specs=[whole] * (2 + outs),
        scratch_shapes=scratch
        + [
            pltpu.VMEM((8, rows, wide), bf16),
            pltpu.VMEM((8, rows, tokens), bf16),
            pltpu.VMEM((8, rows, tokens), bf16),
            pltpu.SemaphoreType.DMA((16 + 3 * len(pieces),)),
        ],
        compiler_params=pltpu.CompilerParams(vmem_limit_bytes=VMEM_LIMIT),
    )(where, spots, x, dy, xt, dyt, *pieces, *(base or ()))


def set_up(keys, queries, bias):
    info = keys[0].T
    allowed = (info[:, 0:1] == queries[0, 0:1]) & (info[:, 1:2] <= queries[0, 1:2])
    bias[...] = jnp.where(allowed, 0.0, masked)


def turned(value):
    return value.astype(f32).T.astype(bf16)


def forward_kernel(count, q_ref, keys, queries, *refs):
    kv_refs, (out_ref, log_ref, bias, key, pair) = refs[:count], refs[count:]

    @pl.when(pl.program_id(1) == 0)
    def _():
        set_up(keys, queries, bias)
        wide = kv_refs[0].shape[1]
        for i, kv_ref in enumerate(kv_refs):
            pair[:, i * wide : (i + 1) * wide] = kv_ref[...]
            key[i * wide : (i + 1) * wide, :] = turned(kv_ref[:HEAD, :])

    scores = jnp.dot(key[...], q_ref[...], preferred_element_type=f32) + bias[...]
    top = jnp.max(scores, axis=0, keepdims=True)
    weights = jnp.exp(scores - top)
    total = jnp.sum(weights, axis=0, keepdims=True)
    summed = jnp.dot(pair[HEAD:, :], weights.astype(bf16), preferred_element_type=f32)
    out_ref[...] = (summed / total).astype(bf16)
    log_ref[0, 0] = top + jnp.log(total)


def backward_kernel(count, q_ref, do_ref, out_ref, log_ref, keys, queries, *refs):
    kv_refs, dq_ref, dkv_refs = refs[:count], refs[count], refs[count + 1 : 2 * count + 1]
    bias, key, val, pair, acc = refs[2 * count + 1 :]
    head = pl.program_id(1)
    wide = kv_refs[0].shape[1]

    @pl.when(head == 0)
    def _():
        set_up(keys, queries, bias)
        for i, kv_ref in enumerate(kv_refs):
            pair[:, i * wide : (i + 1) * wide] = kv_ref[...]
            key[i * wide : (i + 1) * wide, :] = turned(kv_ref[:HEAD, :])
            val[i * wide : (i + 1) * wide, :] = turned(kv_ref[HEAD:, :])
        acc[...] = jnp.zeros_like(acc)

    query, grad = q_ref[...], do_ref[...]
    scores = jnp.dot(key[...], query, preferred_element_type=f32) + bias[...]
    prob = jnp.exp(scores - log_ref[0, 0])
    delta = jnp.sum(grad.astype(f32) * out_ref[...].astype(f32), axis=0, keepdims=True)
    grad_prob = jnp.dot(val[...], grad, preferred_element_type=f32)
    grad_score = (prob * (grad_prob - delta)).astype(bf16)
    dq_ref[...] = jnp.dot(pair[:HEAD, :], grad_score, preferred_element_type=f32)
    acc[:HEAD, :] += contract(query, grad_score, (1, 1))
    acc[HEAD:, :] += contract(grad, prob.astype(bf16), (1, 1))

    @pl.when(head == pl.num_programs(1) - 1)
    def _():
        for i, dkv_ref in enumerate(dkv_refs):
            dkv_ref[...] = acc[:, i * wide : (i + 1) * wide].astype(bf16)


def attention_specs(stretch, wide, length):
    head_block = pl.BlockSpec((HEAD, stretch), lambda s, h: (h, s))
    log_block = pl.BlockSpec((1, 1, 1, stretch), lambda s, h: (s, h, 0, 0))
    kv_block = pl.BlockSpec((2 * HEAD, wide), lambda s, h: (0, s))
    key_block = pl.BlockSpec((1, 8, length), lambda s, h: (s, 0, 0))
    query_block = pl.BlockSpec((1, 8, stretch), lambda s, h: (s, 0, 0))
    return head_block, log_block, kv_block, [key_block, query_block]


def attention_forward(query, blocks, ids, seqs):
    stretch, group = query.shape[1] // seqs, query.shape[0] // HEAD
    wide, length = blocks[0].shape[1] // seqs, ids[0].shape[2]
    head_block, log_block, kv_block, id_blocks = attention_specs(stretch, wide, length)
    return pl.pallas_call(
        functools.partial(forward_kernel, len(blocks)),
        grid=(seqs, group),
        in_specs=[head_block] + id_blocks + [kv_block] * len(blocks),
        out_specs=[head_block, log_block],
        out_shape=[
            jax.ShapeDtypeStruct(query.shape, bf16),
            jax.ShapeDtypeStruct((seqs, group, 1, stretch), f32),
        ],
        scratch_shapes=[
            pltpu.VMEM((length, stretch), f32),
            pltpu.VMEM((length, HEAD), bf16),
            pltpu.VMEM((2 * HEAD, length), bf16),
        ],
        compiler_params=pltpu.CompilerParams(vmem_limit_bytes=VMEM_LIMIT),
    )(query, *ids, *blocks)


def attention_backward(query, grad, attended, logsum, blocks, ids, seqs):
    stretch, group = query.shape[1] // seqs, query.shape[0] // HEAD
    wide, length = blocks[0].shape[1] // seqs, ids[0].shape[2]
    head_block, log_block, kv_block, id_blocks = attention_specs(stretch, wide, length)
    dq, *dkv = pl.pallas_call(
        functools.partial(backward_kernel, len(blocks)),
        grid=(seqs, group),
        in_specs=[head_block, head_block, head_block, log_block] + id_blocks + [kv_block] * len(blocks),
        out_specs=[head_block] + [kv_block] * len(blocks),
        out_shape=[jax.ShapeDtypeStruct(query.shape, f32)]
        + [jax.ShapeDtypeStruct(block.shape, bf16) for block in blocks],
        scratch_shapes=[
            pltpu.VMEM((length, stretch), f32),
            pltpu.VMEM((length, HEAD), bf16),
            pltpu.VMEM((length, HEAD), bf16),
            pltpu.VMEM((2 * HEAD, length), bf16),
            pltpu.VMEM((2 * HEAD, length), f32),
        ],
        compiler_params=pltpu.CompilerParams(vmem_limit_bytes=VMEM_LIMIT),
    )(query, grad, attended, logsum, *ids, *blocks)
    return dq, dkv


def turn(values, cosine, sine, sign):
    feats, tokens = values.shape
    parts = values.reshape(feats // HEAD, 2, HEAD // 2, tokens)
    a, b = parts[:, 0], parts[:, 1]
    s = sine * sign
    return jnp.stack([a * cosine - b * s, b * cosine + a * s], axis=1).reshape(feats, tokens)


def norm_grad(grad, gain, unit, inverse):
    scaled = grad * gain
    return inverse * (scaled - unit * jnp.mean(scaled * unit, axis=-1, keepdims=True))


def local(
    sizes,
    activations,
    segments,
    cotangent,
    query_weight,
    key_weight,
    value_weight,
    out_weight,
    query_bias,
    key_bias_vector,
    value_bias,
    attention_gain,
    gate_weight,
    up_weight,
    down_weight,
    mlp_gain,
):
    dp_size, ctx_size, tensor_size = sizes
    fast = dp_size == 4 and ctx_size == 4
    near_keys = ctx_size <= 4
    micros, per_micro, stretch, width = activations.shape
    seqs = micros * per_micro
    tokens = seqs * stretch
    length = ctx_size * stretch
    qw = query_weight.shape[1]
    units = gate_weight.shape[1]
    scale = HEAD ** (-0.5)
    ctx = lax.axis_index("ctx")

    plain = jnp.arange(8, dtype=jnp.int32)
    where, spots = (gathered_spots(), kept_spots()) if fast else (plain, plain)
    down_rows = down_weight.T
    ends = [0] + [units * share // (19 * 128) * 128 for share in SHARES] + [units]
    cuts = list(zip(ends[:-1], ends[1:]))
    packs = [
        jnp.concatenate([w[:, lo:hi] for w in (gate_weight, up_weight, down_rows)], axis=1) for lo, hi in cuts
    ]
    first = gather_whole(packs[0])
    if fast:
        second = gather_whole(packs[1])
    qkv_shard = jnp.concatenate([query_weight, key_weight, value_weight], axis=1)
    if fast:
        get_qkv = gather_begin(qkv_shard)
        get_out = gather_begin(out_weight.T)
        qkv_blocks = gather_end(get_qkv)
        w_qkv = place(qkv_blocks, where)
    else:
        w_out = gather_whole(out_weight.T)
        w_qkv = gather_whole(qkv_shard)

    own_ids = segments.reshape(seqs, stretch)
    steps = jnp.arange(stretch, dtype=jnp.int32)
    query_pos = ctx * stretch + steps
    if near_keys:
        key_pos = jnp.concatenate([(ctx - r) * stretch + steps for r in range(ctx_size)])
        key_ids = jnp.where(key_pos >= 0, jnp.concatenate(earlier(own_ids, ctx_size), axis=1), -1)
    else:
        key_pos = jnp.arange(length, dtype=jnp.int32)
        key_ids = lax.all_gather(own_ids, "ctx", axis=1, tiled=True)
    before = (key_ids[:, :, None] == own_ids[:, None, :]) & (
        key_pos[None, :, None] < query_pos[None, None, :]
    )
    position = jnp.sum(before.astype(f32), axis=1).reshape(1, tokens)
    freq = theta ** (-(2.0 / HEAD) * jnp.arange(HEAD // 2, dtype=f32))
    angle = freq[:, None] * position
    cosine, sine = jnp.cos(angle), jnp.sin(angle)
    ids = tuple(
        jnp.concatenate(
            [number[:, None], jnp.broadcast_to(place_of, number.shape)[:, None]] + [number[:, None]] * 6, axis=1
        ).astype(f32)
        for number, place_of in ((key_ids, key_pos), (own_ids, query_pos))
    )

    source = activations.reshape(tokens, width).astype(f32)
    inverse1 = lax.rsqrt(jnp.mean(source * source, axis=-1, keepdims=True) + eps)
    unit1 = source * inverse1
    normed1 = (unit1 * attention_gain).astype(bf16)
    bias = jnp.concatenate([query_bias, key_bias_vector, value_bias])
    qkv = contract(w_qkv, normed1, (0, 1)) + bias[:, None]
    query = (turn(qkv[:qw], cosine, sine, 1.0).astype(bf16) * scale).astype(bf16)
    key = turn(qkv[qw : qw + HEAD], cosine, sine, 1.0).astype(bf16)
    pair = jnp.concatenate([key, qkv[qw + HEAD :].astype(bf16)], axis=0)

    def group_of(value, m):
        wide = value.shape[1] // micros
        return value[:, m * wide : (m + 1) * wide]

    def ids_of(m):
        return tuple(v[m * per_micro : (m + 1) * per_micro] for v in ids)

    pairs, attended, logsums = [], [], []
    for m in range(micros):
        mine = group_of(pair, m)
        if near_keys:
            pairs.append(earlier(mine, ctx_size))
        else:
            wide = [
                lax.all_gather(mine[:, i * stretch : (i + 1) * stretch], "ctx", axis=1, tiled=True)
                for i in range(per_micro)
            ]
            pairs.append([jnp.concatenate(wide, axis=1)])
    plan = ()
    if fast:
        plan = (
            ((get_out, ("near", "far", "near1", "near2", "far1", "far2")),),
            ((get_out, ("near3", "far3")),),
        )
    for m in range(micros):
        query_now = group_of(query, m)
        if fast:
            for held, names in plan[min(m, 1)]:
                gather_next(held, *names)
                query_now = hold(query_now, held, names)
        out, logsum = attention_forward(query_now, pairs[m], ids_of(m), per_micro)
        attended.append(out)
        logsums.append(logsum)
    if fast:
        out_blocks = gather_end(get_out)
        w_out = place(out_blocks, where)
    partial = jnp.concatenate([contract(out, w_out, (0, 1)) for out in attended], axis=0)
    mixed = source + tensor_sum(partial, tensor_size)

    inverse2 = lax.rsqrt(jnp.mean(mixed * mixed, axis=-1, keepdims=True) + eps)
    unit2 = mixed * inverse2
    normed2 = (unit2 * mlp_gain).astype(bf16)
    grad_branch = cotangent.reshape(tokens, width)
    grad_result = grad_branch.astype(f32)
    normed2_t, branch_t = (v.T.reshape(8, width // 8, tokens) for v in (normed2, grad_branch))
    shape = (8, width // 8, -1)
    *sums, grads_a = some_units(
        [[first.reshape(shape)]], plain, plain, normed2, grad_branch, normed2_t, branch_t, None, 1
    )
    grads_a = scatter_whole(grads_a.reshape(width, -1))
    if not fast:
        grads_a, pack = lax.optimization_barrier((grads_a, packs[1]))
        second = gather_whole(pack)
    out, dn, *grads_b = some_units(
        [[second.reshape(shape)]], plain, spots, normed2, grad_branch, normed2_t, branch_t, sums, 4 if fast else 1
    )
    sums = [out, dn]
    if fast:
        grads_b = scatter_begin(grads_b)
    result = mixed + tensor_sum(sums[0], tensor_size)
    output = result.astype(bf16).reshape(activations.shape)
    grad_normed2 = tensor_sum(sums[1], tensor_size)
    grad_gain2 = jnp.sum(grad_normed2 * unit2, axis=0)
    grad_mixed = grad_result + norm_grad(grad_normed2, mlp_gain, unit2, inverse2)

    grad_attn = grad_mixed.astype(bf16)
    grad_attended = contract(w_out, grad_attn, (0, 1)).astype(bf16)
    grad_out_w = contract(grad_attn, jnp.concatenate(attended, axis=1), (0, 1))
    grads_c = scatter_begin(in_parts(grad_out_w)) if fast else None
    grad_queries, grad_pairs = [], []
    for m in range(micros):
        grad_now = group_of(grad_attended, m)
        if fast and m == 1:
            grad_now = hold(grad_now, grads_b, ["a1", "b1"])
            scatter_second(grads_b)
        grad_query, grad_blocks = attention_backward(
            group_of(query, m), grad_now, attended[m], logsums[m], pairs[m], ids_of(m), per_micro
        )
        if near_keys:
            own = give_back(grad_blocks, ctx_size)
        else:
            wide = [grad_blocks[0][:, i * length : (i + 1) * length] for i in range(per_micro)]
            own = [lax.psum_scatter(w, "ctx", scatter_dimension=1, tiled=True) for w in wide]
            own = jnp.concatenate(own, axis=1).astype(f32)
        if fast and m == 1:
            grad_query = hold(grad_query, grads_c, ["a1", "b1"])
            scatter_second(grads_c)
        grad_queries.append(grad_query)
        grad_pairs.append(own.reshape(2 * HEAD, per_micro * stretch))
    grad_query = jnp.concatenate(grad_queries, axis=1) * scale
    grad_pair = jnp.concatenate(grad_pairs, axis=1)
    grad_qkv = jnp.concatenate(
        [
            turn(grad_query, cosine, sine, -1.0),
            turn(grad_pair[:HEAD], cosine, sine, -1.0),
            grad_pair[HEAD:],
        ],
        axis=0,
    ).astype(bf16)
    grad_bias = jnp.sum(grad_qkv.astype(f32), axis=1)
    grad_qkv_w = contract(normed1, grad_qkv, (0, 1))
    if fast:
        parts = in_parts(grad_qkv_w)
        grad_qkv, *parts = lax.optimization_barrier((grad_qkv, *parts))
        grads_d = scatter_begin(parts)
        for held in (grads_b, grads_c):
            grad_qkv = hold(grad_qkv, held, ["a2", "b2"])
            scatter_third(held)
    grad_normed1 = tensor_sum(contract(grad_qkv, w_qkv, (0, 1)), tensor_size)
    grad_gain1 = jnp.sum(grad_normed1 * unit1, axis=0)
    grad_source = grad_mixed + norm_grad(grad_normed1, attention_gain, unit1, inverse1)

    if fast:
        for held in (grads_b, grads_c):
            grad_source = hold(grad_source, held, ["c1", "c2", "c3"])
        grad_units = [grads_a, scatter_end(grads_b)]
        grad_out_w, grad_qkv_w = scatter_end(grads_c), scatter_end(grads_d)
    else:
        grad_units = [grads_a, scatter_whole(grads_b[0].reshape(width, -1))]
        grad_out_w, grad_qkv_w = (scatter_whole(g.astype(bf16)) for g in (grad_out_w, grad_qkv_w))
    grad_gate_w, grad_up_w, grad_down = (
        jnp.concatenate(
            [g[:, m * (hi - lo) : (m + 1) * (hi - lo)] for g, (lo, hi) in zip(grad_units, cuts)], axis=1
        )
        for m in range(3)
    )

    smalls = sum_small(jnp.concatenate([grad_bias, grad_gain1, grad_gain2]), fast)
    ends = [qw, qw + HEAD, qw + 2 * HEAD, qw + 2 * HEAD + width]
    small = jnp.split(smalls, ends)
    return (
        output,
        grad_source.reshape(activations.shape),
        grad_qkv_w[:, :qw],
        grad_qkv_w[:, qw : qw + HEAD],
        grad_qkv_w[:, qw + HEAD :],
        grad_out_w.T,
        small[0],
        small[1],
        small[2],
        small[3],
        grad_gate_w,
        grad_up_w,
        grad_down.T,
        small[4],
    )


def solution(mesh):
    sizes = (mesh.shape["dp"], mesh.shape["ctx"], mesh.shape["tensor"])
    return jax.shard_map(
        functools.partial(local, sizes),
        mesh=mesh,
        in_specs=(
            P(None, "dp", "ctx", None),
            P(None, "dp", "ctx"),
            P(None, "dp", "ctx", None),
            P(("dp", "ctx"), "tensor"),
            P(("dp", "ctx"), "tensor"),
            P(("dp", "ctx"), "tensor"),
            P("tensor", ("dp", "ctx")),
            P("tensor"),
            P("tensor"),
            P("tensor"),
            P(),
            P(("dp", "ctx"), "tensor"),
            P(("dp", "ctx"), "tensor"),
            P("tensor", ("dp", "ctx")),
            P(),
        ),
        out_specs=(
            P(None, "dp", "ctx", None),
            P(None, "dp", "ctx", None),
            P(("dp", "ctx"), "tensor"),
            P(("dp", "ctx"), "tensor"),
            P(("dp", "ctx"), "tensor"),
            P("tensor", ("dp", "ctx")),
            P("tensor"),
            P("tensor"),
            P("tensor"),
            P(),
            P(("dp", "ctx"), "tensor"),
            P(("dp", "ctx"), "tensor"),
            P("tensor", ("dp", "ctx")),
            P(),
        ),
        check_vma=False,
    )
```

```python
import functools

import jax
import jax.numpy as jnp
from jax import lax
from jax.experimental import pallas as pl
from jax.experimental.pallas import tpu as pltpu
from jax.sharding import PartitionSpec as P

HEAD = 64

eps = 1e-06
theta = 1000000.0
masked = -1e30
f32 = jnp.float32
bf16 = jnp.bfloat16
VMEM_LIMIT = 56 * 1024 * 1024


def contract(left, right, dims):
    return lax.dot_general(left, right, ((dims[:1], dims[1:]), ((), ())), preferred_element_type=f32)


def swap(value, axis, size, bit):
    return lax.ppermute(value, axis, [(i, i ^ bit) for i in range(size)])


def tensor_sum(partial, size):
    sent = partial.astype(bf16)
    if size == 2:
        return sent.astype(f32) + swap(sent, "tensor", 2, 1).astype(f32)
    return lax.psum(sent, "tensor").astype(f32)


def pair_of(dp, ctx):
    return dp * 2 + ctx // 2


def hold(value, held, names):
    names = [name for name in names if name in held]
    value, *got = lax.optimization_barrier((value,) + tuple(held[name] for name in names))
    held.update(zip(names, got))
    return value


def gather_whole(shard):
    return lax.all_gather(shard, ("dp", "ctx"), axis=0, tiled=True)


def scatter_whole(total):
    return lax.psum_scatter(total, ("dp", "ctx"), scatter_dimension=0, tiled=True).astype(f32)


def gather_begin(shard):
    held = {"z%d" % k: swap(shard, "ctx", 4, k) for k in (1, 2, 3)}
    held["own"] = shard
    return held


BLOCKS = ("near", "near1", "near2", "near3", "far", "far1", "far2", "far3")


def gather_next(held, *names):
    def in_order(one, two):
        even = lax.axis_index("ctx") % 2 == 0
        return jnp.concatenate([jnp.where(even, one, two), jnp.where(even, two, one)], axis=0)

    for name in names:
        if name in held:
            continue
        if name == "near":
            held[name] = in_order(held["own"], held["z1"])
        elif name == "far":
            held[name] = in_order(held["z2"], held["z3"])
        else:
            source, bit = {
                "near1": ("near", 1),
                "near2": ("near", 2),
                "near3": ("near1", 2),
                "far1": ("far", 1),
                "far2": ("far", 2),
                "far3": ("far2", 1),
            }[name]
            held[name] = swap(held[source], "dp", 4, bit)


def gather_end(held):
    gather_next(held, *BLOCKS)
    return [held[name] for name in BLOCKS]


def gathered_spots():
    me = pair_of(lax.axis_index("dp"), lax.axis_index("ctx"))
    return jnp.stack([me ^ (k * 2 + h) for h in (0, 1) for k in (0, 1, 2, 3)]).astype(jnp.int32)


def kept_spots():
    me = pair_of(lax.axis_index("dp"), lax.axis_index("ctx"))
    order = (0, 2, 4, 6, 1, 5, 3, 7)
    return jnp.stack([me ^ r for r in order]).astype(jnp.int32)


def place_kernel(where_ref, *refs):
    count = len(refs) - 2
    pieces, out_ref, sems = refs[:count], refs[count], refs[count + 1]
    copies = [
        pltpu.make_async_copy(pieces[i], out_ref.at[where_ref[i]], sems.at[i]) for i in range(count)
    ]
    for copy in copies:
        copy.start()
    for copy in copies:
        copy.wait()


def place(pieces, where):
    count = len(pieces)
    whole = pl.pallas_call(
        place_kernel,
        out_shape=jax.ShapeDtypeStruct((count,) + pieces[0].shape, pieces[0].dtype),
        in_specs=[pl.BlockSpec(memory_space=pltpu.SMEM)] + [pl.BlockSpec(memory_space=pl.ANY)] * count,
        out_specs=pl.BlockSpec(memory_space=pltpu.VMEM),
        scratch_shapes=[pltpu.SemaphoreType.DMA((count,))],
        compiler_params=pltpu.CompilerParams(vmem_limit_bytes=VMEM_LIMIT),
    )(where, *pieces)
    return whole.reshape(count * pieces[0].shape[0], pieces[0].shape[1])


def add16(left, right):
    return (left.astype(f32) + right.astype(f32)).astype(bf16)


def scatter_begin(parts):
    keep_a, send_a, keep_b, send_b = parts
    return {"keep": (keep_a, keep_b), "a1": swap(send_a, "dp", 4, 2), "b1": swap(send_b, "dp", 4, 1)}


def scatter_second(held):
    keep_a, keep_b = held["keep"]
    a, b = held["a1"], held["b1"]
    held["a2"] = swap(add16(keep_a[1], a[1]), "dp", 4, 1)
    held["b2"] = swap(add16(keep_b[1], b[1]), "dp", 4, 2)
    held["left"] = add16(keep_a[0], a[0]), add16(keep_b[0], b[0])


def scatter_third(held):
    left_a, left_b = held["left"]
    near, far = add16(left_a, held["a2"]), add16(left_b, held["b2"])
    odd = lax.axis_index("ctx") % 2

    def half_of(value, at):
        rows = value.shape[0] // 2
        return lax.dynamic_slice_in_dim(value, at * rows, rows, 0)

    held["mine"] = half_of(near, odd)
    held["c1"] = swap(half_of(near, 1 - odd), "ctx", 4, 1)
    held["c2"] = swap(half_of(far, odd), "ctx", 4, 2)
    held["c3"] = swap(half_of(far, 1 - odd), "ctx", 4, 3)


def scatter_end(held):
    if "a2" not in held:
        scatter_second(held)
    if "c1" not in held:
        scatter_third(held)
    total = held["mine"].astype(f32)
    for name in ("c1", "c2", "c3"):
        total = total + held[name].astype(f32)
    return total


def in_parts(total):
    cut, spots = total.astype(bf16).reshape(8, -1, total.shape[1]), kept_spots()
    block = [lax.dynamic_index_in_dim(cut, spots[i], 0) for i in range(8)]
    return [jnp.concatenate(block[2 * i : 2 * i + 2]) for i in range(4)]


def sum_small(value, fast):
    if not fast:
        return lax.psum(value, ("dp", "ctx"))
    for axis, bit in (("ctx", 1), ("ctx", 2), ("dp", 1), ("dp", 2)):
        value = value + swap(value, axis, 4, bit)
    return value


def earlier(value, ctx_size):
    return [value] + [
        lax.ppermute(value, "ctx", [(i, i + back) for i in range(ctx_size - back)])
        for back in range(1, ctx_size)
    ]


def give_back(blocks, ctx_size):
    total = blocks[0].astype(f32)
    for back in range(1, ctx_size):
        total = total + lax.ppermute(
            blocks[back], "ctx", [(i + back, i) for i in range(ctx_size - back)]
        ).astype(f32)
    return total


def units_kernel(counts, parts, has_base, outs, where, spots, x_ref, dy_ref, xt_ref, dyt_ref, *refs):
    pieces, refs = refs[: sum(parts)], refs[sum(parts) :]
    if has_base:
        base, refs = refs[:2], refs[2:]
    out_ref, dn_ref, *refs = refs
    grads, refs = refs[:outs], refs[outs:]
    if has_base:
        (acc_out, acc_dn), refs = refs[:2], refs[2:]
    else:
        acc_out, acc_dn = out_ref, dn_ref
    weights, xt, dyt, sems = refs
    count = sum(counts)
    moves = []
    for i in range(8):
        moves.append((xt_ref.at[spots[i]], xt.at[i]))
        moves.append((dyt_ref.at[spots[i]], dyt.at[i]))
    taken, begin = 0, 0
    for part, units in zip(parts, counts):
        for m in range(3):
            there, here = pl.ds(m * units, units), pl.ds(m * count + begin, units)
            for i in range(part):
                if part == 1:
                    moves.append((pieces[taken].at[:, :, there], weights.at[:, :, here]))
                else:
                    moves.append((pieces[taken + i].at[:, there], weights.at[where[i], :, here]))
        taken, begin = taken + part, begin + units
    copies = [pltpu.make_async_copy(a, b, sems.at[i]) for i, (a, b) in enumerate(moves)]
    for copy in copies:
        copy.start()
    if has_base:
        acc_out[...] = base[0][...]
        acc_dn[...] = base[1][...]
    else:
        acc_out[...] = jnp.zeros_like(acc_out)
        acc_dn[...] = jnp.zeros_like(acc_dn)
    for copy in copies:
        copy.wait()
    depth = x_ref.shape[1]

    def weight(m, start, size):
        return weights[:, :, pl.ds(m * count + start, size)].reshape(depth, size)

    def some_units(start, size):
        w_gate, w_up, w_down = (weight(m, start, size) for m in range(3))
        gate = jnp.dot(x_ref[...], w_gate, preferred_element_type=f32)
        up = jnp.dot(x_ref[...], w_up, preferred_element_type=f32)
        d_hidden = jnp.dot(dy_ref[...], w_down, preferred_element_type=f32)
        sigma = jax.nn.sigmoid(gate)
        silu = gate * sigma
        hidden = (silu * up).astype(bf16)
        d_gate = (d_hidden * up * (sigma * (1.0 + gate * (1.0 - sigma)))).astype(bf16)
        d_up = (d_hidden * silu).astype(bf16)
        acc_out[...] += contract(hidden, w_down, (1, 1))
        acc_dn[...] += contract(d_gate, w_gate, (1, 1)) + contract(d_up, w_up, (1, 1))
        for m, (left, right) in enumerate(((xt, d_gate), (xt, d_up), (dyt, hidden))):
            grad = jnp.dot(
                left[...].reshape(depth, left.shape[2]), right, preferred_element_type=f32
            ).astype(bf16).reshape(8, depth // 8, size)
            for i, grad_ref in enumerate(grads):
                each = 8 // outs
                grad_ref[:, :, pl.ds(m * count + start, size)] = grad[each * i : each * i + each]

    wide = UNIT_TILE
    full = count // wide

    @pl.loop(0, full)
    def _(step):
        some_units(pl.multiple_of(step * wide, 128), wide)

    if count % wide:
        some_units(full * wide, count % wide)
    if has_base:
        out_ref[...] = acc_out[...].astype(out_ref.dtype)
        dn_ref[...] = acc_dn[...].astype(dn_ref.dtype)


UNIT_TILE = 256
SHARES = (8,)


def some_units(packs, where, spots, x, dy, xt, dyt, base, outs):
    tokens, depth = x.shape
    rows = depth // 8
    counts = [pack[0].shape[-1] // 3 for pack in packs]
    parts = [len(pack) for pack in packs]
    pieces = [piece for pack in packs for piece in pack]
    wide = 3 * sum(counts)
    whole = pl.BlockSpec(memory_space=pltpu.VMEM)
    smem = pl.BlockSpec(memory_space=pltpu.SMEM)
    anywhere = pl.BlockSpec(memory_space=pl.ANY)
    has_base = base is not None
    sums = jax.ShapeDtypeStruct((tokens, depth), bf16 if has_base else f32)
    grad = jax.ShapeDtypeStruct((8 // outs, rows, wide), bf16)
    scratch = [pltpu.VMEM((tokens, depth), f32)] * 2 if has_base else []
    return pl.pallas_call(
        functools.partial(units_kernel, counts, parts, has_base, outs),
        out_shape=[sums, sums] + [grad] * outs,
        in_specs=[smem, smem, whole, whole] + [anywhere] * (2 + len(pieces)) + ([whole] * 2 if has_base else []),
        out_specs=[whole] * (2 + outs),
        scratch_shapes=scratch
        + [
            pltpu.VMEM((8, rows, wide), bf16),
            pltpu.VMEM((8, rows, tokens), bf16),
            pltpu.VMEM((8, rows, tokens), bf16),
            pltpu.SemaphoreType.DMA((16 + 3 * len(pieces),)),
        ],
        compiler_params=pltpu.CompilerParams(vmem_limit_bytes=VMEM_LIMIT),
    )(where, spots, x, dy, xt, dyt, *pieces, *(base or ()))


def set_up(keys, queries, bias):
    info = keys[0].T
    allowed = (info[:, 0:1] == queries[0, 0:1]) & (info[:, 1:2] <= queries[0, 1:2])
    bias[...] = jnp.where(allowed, 0.0, masked)


def turned(value):
    return value.astype(f32).T.astype(bf16)


def forward_kernel(count, q_ref, keys, queries, *refs):
    kv_refs, (out_ref, log_ref, bias, key, pair) = refs[:count], refs[count:]

    @pl.when(pl.program_id(1) == 0)
    def _():
        set_up(keys, queries, bias)
        wide = kv_refs[0].shape[1]
        for i, kv_ref in enumerate(kv_refs):
            pair[:, i * wide : (i + 1) * wide] = kv_ref[...]
            key[i * wide : (i + 1) * wide, :] = turned(kv_ref[:HEAD, :])

    scores = jnp.dot(key[...], q_ref[...], preferred_element_type=f32) + bias[...]
    top = jnp.max(scores, axis=0, keepdims=True)
    weights = jnp.exp(scores - top)
    total = jnp.sum(weights, axis=0, keepdims=True)
    summed = jnp.dot(pair[HEAD:, :], weights.astype(bf16), preferred_element_type=f32)
    out_ref[...] = (summed / total).astype(bf16)
    log_ref[0, 0] = top + jnp.log(total)


def backward_kernel(count, q_ref, do_ref, out_ref, log_ref, keys, queries, *refs):
    kv_refs, dq_ref, dkv_refs = refs[:count], refs[count], refs[count + 1 : 2 * count + 1]
    bias, key, val, pair, acc = refs[2 * count + 1 :]
    head = pl.program_id(1)
    wide = kv_refs[0].shape[1]

    @pl.when(head == 0)
    def _():
        set_up(keys, queries, bias)
        for i, kv_ref in enumerate(kv_refs):
            pair[:, i * wide : (i + 1) * wide] = kv_ref[...]
            key[i * wide : (i + 1) * wide, :] = turned(kv_ref[:HEAD, :])
            val[i * wide : (i + 1) * wide, :] = turned(kv_ref[HEAD:, :])
        acc[...] = jnp.zeros_like(acc)

    query, grad = q_ref[...], do_ref[...]
    scores = jnp.dot(key[...], query, preferred_element_type=f32) + bias[...]
    prob = jnp.exp(scores - log_ref[0, 0])
    delta = jnp.sum(grad.astype(f32) * out_ref[...].astype(f32), axis=0, keepdims=True)
    grad_prob = jnp.dot(val[...], grad, preferred_element_type=f32)
    grad_score = (prob * (grad_prob - delta)).astype(bf16)
    dq_ref[...] = jnp.dot(pair[:HEAD, :], grad_score, preferred_element_type=f32)
    acc[:HEAD, :] += contract(query, grad_score, (1, 1))
    acc[HEAD:, :] += contract(grad, prob.astype(bf16), (1, 1))

    @pl.when(head == pl.num_programs(1) - 1)
    def _():
        for i, dkv_ref in enumerate(dkv_refs):
            dkv_ref[...] = acc[:, i * wide : (i + 1) * wide].astype(bf16)


def attention_specs(stretch, wide, length):
    head_block = pl.BlockSpec((HEAD, stretch), lambda s, h: (h, s))
    log_block = pl.BlockSpec((1, 1, 1, stretch), lambda s, h: (s, h, 0, 0))
    kv_block = pl.BlockSpec((2 * HEAD, wide), lambda s, h: (0, s))
    key_block = pl.BlockSpec((1, 8, length), lambda s, h: (s, 0, 0))
    query_block = pl.BlockSpec((1, 8, stretch), lambda s, h: (s, 0, 0))
    return head_block, log_block, kv_block, [key_block, query_block]


def attention_forward(query, blocks, ids, seqs):
    stretch, group = query.shape[1] // seqs, query.shape[0] // HEAD
    wide, length = blocks[0].shape[1] // seqs, ids[0].shape[2]
    head_block, log_block, kv_block, id_blocks = attention_specs(stretch, wide, length)
    return pl.pallas_call(
        functools.partial(forward_kernel, len(blocks)),
        grid=(seqs, group),
        in_specs=[head_block] + id_blocks + [kv_block] * len(blocks),
        out_specs=[head_block, log_block],
        out_shape=[
            jax.ShapeDtypeStruct(query.shape, bf16),
            jax.ShapeDtypeStruct((seqs, group, 1, stretch), f32),
        ],
        scratch_shapes=[
            pltpu.VMEM((length, stretch), f32),
            pltpu.VMEM((length, HEAD), bf16),
            pltpu.VMEM((2 * HEAD, length), bf16),
        ],
        compiler_params=pltpu.CompilerParams(vmem_limit_bytes=VMEM_LIMIT),
    )(query, *ids, *blocks)


def attention_backward(query, grad, attended, logsum, blocks, ids, seqs):
    stretch, group = query.shape[1] // seqs, query.shape[0] // HEAD
    wide, length = blocks[0].shape[1] // seqs, ids[0].shape[2]
    head_block, log_block, kv_block, id_blocks = attention_specs(stretch, wide, length)
    dq, *dkv = pl.pallas_call(
        functools.partial(backward_kernel, len(blocks)),
        grid=(seqs, group),
        in_specs=[head_block, head_block, head_block, log_block] + id_blocks + [kv_block] * len(blocks),
        out_specs=[head_block] + [kv_block] * len(blocks),
        out_shape=[jax.ShapeDtypeStruct(query.shape, f32)]
        + [jax.ShapeDtypeStruct(block.shape, bf16) for block in blocks],
        scratch_shapes=[
            pltpu.VMEM((length, stretch), f32),
            pltpu.VMEM((length, HEAD), bf16),
            pltpu.VMEM((length, HEAD), bf16),
            pltpu.VMEM((2 * HEAD, length), bf16),
            pltpu.VMEM((2 * HEAD, length), f32),
        ],
        compiler_params=pltpu.CompilerParams(vmem_limit_bytes=VMEM_LIMIT),
    )(query, grad, attended, logsum, *ids, *blocks)
    return dq, dkv


def turn(values, cosine, sine, sign):
    feats, tokens = values.shape
    parts = values.reshape(feats // HEAD, 2, HEAD // 2, tokens)
    a, b = parts[:, 0], parts[:, 1]
    s = sine * sign
    return jnp.stack([a * cosine - b * s, b * cosine + a * s], axis=1).reshape(feats, tokens)


def norm_grad(grad, gain, unit, inverse):
    scaled = grad * gain
    return inverse * (scaled - unit * jnp.mean(scaled * unit, axis=-1, keepdims=True))


def local(
    sizes,
    activations,
    segments,
    cotangent,
    query_weight,
    key_weight,
    value_weight,
    out_weight,
    query_bias,
    key_bias_vector,
    value_bias,
    attention_gain,
    gate_weight,
    up_weight,
    down_weight,
    mlp_gain,
):
    dp_size, ctx_size, tensor_size = sizes
    fast = dp_size == 4 and ctx_size == 4
    near_keys = ctx_size <= 4
    micros, per_micro, stretch, width = activations.shape
    seqs = micros * per_micro
    tokens = seqs * stretch
    length = ctx_size * stretch
    qw = query_weight.shape[1]
    units = gate_weight.shape[1]
    scale = HEAD ** (-0.5)
    ctx = lax.axis_index("ctx")

    plain = jnp.arange(8, dtype=jnp.int32)
    where, spots = (gathered_spots(), kept_spots()) if fast else (plain, plain)
    down_rows = down_weight.T
    ends = [0] + [units * share // (19 * 128) * 128 for share in SHARES] + [units]
    cuts = list(zip(ends[:-1], ends[1:]))
    packs = [
        jnp.concatenate([w[:, lo:hi] for w in (gate_weight, up_weight, down_rows)], axis=1) for lo, hi in cuts
    ]
    first = gather_whole(packs[0])
    if fast:
        second = gather_whole(packs[1])
    qkv_shard = jnp.concatenate([query_weight, key_weight, value_weight], axis=1)
    if fast:
        get_qkv = gather_begin(qkv_shard)
        get_out = gather_begin(out_weight.T)
        qkv_blocks = gather_end(get_qkv)
        w_qkv = place(qkv_blocks, where)
    else:
        w_out = gather_whole(out_weight.T)
        w_qkv = gather_whole(qkv_shard)

    own_ids = segments.reshape(seqs, stretch)
    steps = jnp.arange(stretch, dtype=jnp.int32)
    query_pos = ctx * stretch + steps
    if near_keys:
        key_pos = jnp.concatenate([(ctx - r) * stretch + steps for r in range(ctx_size)])
        key_ids = jnp.where(key_pos >= 0, jnp.concatenate(earlier(own_ids, ctx_size), axis=1), -1)
    else:
        key_pos = jnp.arange(length, dtype=jnp.int32)
        key_ids = lax.all_gather(own_ids, "ctx", axis=1, tiled=True)
    before = (key_ids[:, :, None] == own_ids[:, None, :]) & (
        key_pos[None, :, None] < query_pos[None, None, :]
    )
    position = jnp.sum(before.astype(f32), axis=1).reshape(1, tokens)
    freq = theta ** (-(2.0 / HEAD) * jnp.arange(HEAD // 2, dtype=f32))
    angle = freq[:, None] * position
    cosine, sine = jnp.cos(angle), jnp.sin(angle)
    ids = tuple(
        jnp.concatenate(
            [number[:, None], jnp.broadcast_to(place_of, number.shape)[:, None]] + [number[:, None]] * 6, axis=1
        ).astype(f32)
        for number, place_of in ((key_ids, key_pos), (own_ids, query_pos))
    )

    source = activations.reshape(tokens, width).astype(f32)
    inverse1 = lax.rsqrt(jnp.mean(source * source, axis=-1, keepdims=True) + eps)
    unit1 = source * inverse1
    normed1 = (unit1 * attention_gain).astype(bf16)
    bias = jnp.concatenate([query_bias, key_bias_vector, value_bias])
    qkv = contract(w_qkv, normed1, (0, 1)) + bias[:, None]
    query = (turn(qkv[:qw], cosine, sine, 1.0).astype(bf16) * scale).astype(bf16)
    key = turn(qkv[qw : qw + HEAD], cosine, sine, 1.0).astype(bf16)
    pair = jnp.concatenate([key, qkv[qw + HEAD :].astype(bf16)], axis=0)

    def group_of(value, m):
        wide = value.shape[1] // micros
        return value[:, m * wide : (m + 1) * wide]

    def ids_of(m):
        return tuple(v[m * per_micro : (m + 1) * per_micro] for v in ids)

    pairs, attended, logsums = [], [], []
    for m in range(micros):
        mine = group_of(pair, m)
        if near_keys:
            pairs.append(earlier(mine, ctx_size))
        else:
            wide = [
                lax.all_gather(mine[:, i * stretch : (i + 1) * stretch], "ctx", axis=1, tiled=True)
                for i in range(per_micro)
            ]
            pairs.append([jnp.concatenate(wide, axis=1)])
    plan = ()
    if fast:
        plan = (
            ((get_out, ("near", "far", "near1", "near2", "far1", "far2")),),
            ((get_out, ("near3", "far3")),),
        )
    for m in range(micros):
        query_now = group_of(query, m)
        if fast:
            for held, names in plan[min(m, 1)]:
                gather_next(held, *names)
                query_now = hold(query_now, held, names)
        out, logsum = attention_forward(query_now, pairs[m], ids_of(m), per_micro)
        attended.append(out)
        logsums.append(logsum)
    if fast:
        out_blocks = gather_end(get_out)
        w_out = place(out_blocks, where)
    partial = jnp.concatenate([contract(out, w_out, (0, 1)) for out in attended], axis=0)
    mixed = source + tensor_sum(partial, tensor_size)

    inverse2 = lax.rsqrt(jnp.mean(mixed * mixed, axis=-1, keepdims=True) + eps)
    unit2 = mixed * inverse2
    normed2 = (unit2 * mlp_gain).astype(bf16)
    grad_branch = cotangent.reshape(tokens, width)
    grad_result = grad_branch.astype(f32)
    normed2_t, branch_t = (v.T.reshape(8, width // 8, tokens) for v in (normed2, grad_branch))
    shape = (8, width // 8, -1)
    *sums, grads_a = some_units(
        [[first.reshape(shape)]], plain, plain, normed2, grad_branch, normed2_t, branch_t, None, 1
    )
    grads_a = scatter_whole(grads_a.reshape(width, -1))
    if not fast:
        grads_a, pack = lax.optimization_barrier((grads_a, packs[1]))
        second = gather_whole(pack)
    out, dn, *grads_b = some_units(
        [[second.reshape(shape)]], plain, spots, normed2, grad_branch, normed2_t, branch_t, sums, 4 if fast else 1
    )
    sums = [out, dn]
    if fast:
        grads_b = scatter_begin(grads_b)
    result = mixed + tensor_sum(sums[0], tensor_size)
    output = result.astype(bf16).reshape(activations.shape)
    grad_normed2 = tensor_sum(sums[1], tensor_size)
    grad_gain2 = jnp.sum(grad_normed2 * unit2, axis=0)
    grad_mixed = grad_result + norm_grad(grad_normed2, mlp_gain, unit2, inverse2)

    grad_attn = grad_mixed.astype(bf16)
    grad_attended = contract(w_out, grad_attn, (0, 1)).astype(bf16)
    grad_out_w = contract(grad_attn, jnp.concatenate(attended, axis=1), (0, 1))
    grads_c = scatter_begin(in_parts(grad_out_w)) if fast else None
    grad_queries, grad_pairs = [], []
    for m in range(micros):
        grad_now = group_of(grad_attended, m)
        if fast and m == 1:
            grad_now = hold(grad_now, grads_b, ["a1", "b1"])
            scatter_second(grads_b)
        grad_query, grad_blocks = attention_backward(
            group_of(query, m), grad_now, attended[m], logsums[m], pairs[m], ids_of(m), per_micro
        )
        if near_keys:
            own = give_back(grad_blocks, ctx_size)
        else:
            wide = [grad_blocks[0][:, i * length : (i + 1) * length] for i in range(per_micro)]
            own = [lax.psum_scatter(w, "ctx", scatter_dimension=1, tiled=True) for w in wide]
            own = jnp.concatenate(own, axis=1).astype(f32)
        if fast and m == 1:
            grad_query = hold(grad_query, grads_c, ["a1", "b1"])
            scatter_second(grads_c)
        grad_queries.append(grad_query)
        grad_pairs.append(own.reshape(2 * HEAD, per_micro * stretch))
    grad_query = jnp.concatenate(grad_queries, axis=1) * scale
    grad_pair = jnp.concatenate(grad_pairs, axis=1)
    if fast:
        grad_pair = hold(grad_pair, grads_b, ["a2", "b2"])
        scatter_third(grads_b)
    grad_qkv = jnp.concatenate(
        [
            turn(grad_query, cosine, sine, -1.0),
            turn(grad_pair[:HEAD], cosine, sine, -1.0),
            grad_pair[HEAD:],
        ],
        axis=0,
    ).astype(bf16)
    grad_bias = jnp.sum(grad_qkv.astype(f32), axis=1)
    grad_qkv_w = contract(normed1, grad_qkv, (0, 1))
    if fast:
        parts = in_parts(grad_qkv_w)
        grad_qkv, *parts = lax.optimization_barrier((grad_qkv, *parts))
        grads_d = scatter_begin(parts)
        grad_qkv = hold(grad_qkv, grads_c, ["a2", "b2"])
        scatter_third(grads_c)
    grad_normed1 = tensor_sum(contract(grad_qkv, w_qkv, (0, 1)), tensor_size)
    grad_gain1 = jnp.sum(grad_normed1 * unit1, axis=0)
    grad_source = grad_mixed + norm_grad(grad_normed1, attention_gain, unit1, inverse1)

    smalls = sum_small(jnp.concatenate([grad_bias, grad_gain1, grad_gain2]), fast)
    if fast:
        scatter_second(grads_d)
        for held in (grads_b, grads_c):
            grads_d["a2"] = hold(grads_d["a2"], held, ["c1", "c2", "c3"])
        grads_d["a2"], grad_source, smalls = lax.optimization_barrier((grads_d["a2"], grad_source, smalls))
        grad_units = [grads_a, scatter_end(grads_b)]
        grad_out_w, grad_qkv_w = scatter_end(grads_c), scatter_end(grads_d)
    else:
        grad_units = [grads_a, scatter_whole(grads_b[0].reshape(width, -1))]
        grad_out_w, grad_qkv_w = (scatter_whole(g.astype(bf16)) for g in (grad_out_w, grad_qkv_w))
    grad_gate_w, grad_up_w, grad_down = (
        jnp.concatenate(
            [g[:, m * (hi - lo) : (m + 1) * (hi - lo)] for g, (lo, hi) in zip(grad_units, cuts)], axis=1
        )
        for m in range(3)
    )

    ends = [qw, qw + HEAD, qw + 2 * HEAD, qw + 2 * HEAD + width]
    small = jnp.split(smalls, ends)
    return (
        output,
        grad_source.reshape(activations.shape),
        grad_qkv_w[:, :qw],
        grad_qkv_w[:, qw : qw + HEAD],
        grad_qkv_w[:, qw + HEAD :],
        grad_out_w.T,
        small[0],
        small[1],
        small[2],
        small[3],
        grad_gate_w,
        grad_up_w,
        grad_down.T,
        small[4],
    )


def solution(mesh):
    sizes = (mesh.shape["dp"], mesh.shape["ctx"], mesh.shape["tensor"])
    return jax.shard_map(
        functools.partial(local, sizes),
        mesh=mesh,
        in_specs=(
            P(None, "dp", "ctx", None),
            P(None, "dp", "ctx"),
            P(None, "dp", "ctx", None),
            P(("dp", "ctx"), "tensor"),
            P(("dp", "ctx"), "tensor"),
            P(("dp", "ctx"), "tensor"),
            P("tensor", ("dp", "ctx")),
            P("tensor"),
            P("tensor"),
            P("tensor"),
            P(),
            P(("dp", "ctx"), "tensor"),
            P(("dp", "ctx"), "tensor"),
            P("tensor", ("dp", "ctx")),
            P(),
        ),
        out_specs=(
            P(None, "dp", "ctx", None),
            P(None, "dp", "ctx", None),
            P(("dp", "ctx"), "tensor"),
            P(("dp", "ctx"), "tensor"),
            P(("dp", "ctx"), "tensor"),
            P("tensor", ("dp", "ctx")),
            P("tensor"),
            P("tensor"),
            P("tensor"),
            P(),
            P(("dp", "ctx"), "tensor"),
            P(("dp", "ctx"), "tensor"),
            P("tensor", ("dp", "ctx")),
            P(),
        ),
        check_vma=False,
    )
```
